256 devices in a mesh: grp: 16 (over y_lo, z), sp: 16 (over y_hi, x, core).
Axes of the slice: x: 4, y: 4 (y_hi: 2, y_lo: 2; y = y_hi * 2 + y_lo), z: 8, core: 2. Of those that a mesh axis runs over, the one named last changes fastest.
Arguments:
- queries: bfloat16 [32768, 5120], P(('grp', 'sp')), may hold values from -8 to 8
- keys: bfloat16 [32768, 1024], P(('grp', 'sp')), may hold values from -8 to 8
- values: bfloat16 [32768, 1024], P(('grp', 'sp')), may hold values from -6 to 6
- slot_order: int32 [16, 16, 128], P('grp', 'sp'), may hold values from 0 to 127, each once within a row
- doc_ids: int32 [16, 2048], P('grp'), may hold values from 0 to 3, never falling along the last dimension, each value on 1 to 1024 neighbouring positions
Outputs:
- attended: bfloat16 [32768, 5120], P(('grp', 'sp'))
The draws below stay inside these ranges and needn't reach their ends.
Inputs may be any that keep to these rules, and one draw needn't show every extreme that they name: `slot_order`: each row of the last dimension is a permutation. `doc_ids`: never falling along a group's positions; every document spans at most 1024 positions, and some document spans exactly 1024.
All inputs are finite; a program needn't handle non-finite values.
Results may differ from the reference program's by a relative error of at most 0.0027.
Values may be sent and summed in bfloat16 or wider, within the bound.
No kernel may reach another device: no remote copies, remote signals or barrier semaphores. Data moves between devices by JAX's collectives and lax.ppermute only.
A program may use at most 128 MiB of HBM per device.

```python
import math
import jax
import jax.numpy as jnp
import numpy as np
from jax import lax

QH = 40
KVH = 8
HD = 128
TOK_DEV = 128
DOCS = 4
SPAN = 8
MAXDOC = 1024
GROUP_TOK = 2048
TOKENS = 32768
QW = 5120
KW = 1024
N_GRP = 16
N_SP = 16


def draw_queries(key, part):
    key = jax.random.fold_in(key, 11)
    first, second = jax.random.split(key)
    gauss_part = jax.random.normal(first, (TOKENS, KVH, QH // KVH, HD), jnp.float32)
    row_scale = jnp.exp(jax.random.uniform(second, (TOKENS, 1, 1, 1), jnp.float32, -0.7, 0.7))
    result = row_scale * gauss_part
    return jnp.clip(result, -8.0, 8.0).reshape(TOKENS, QH * HD).astype(jnp.bfloat16)


def draw_keys(key, part):
    key = jax.random.fold_in(key, 23)
    first, second = jax.random.split(key)
    gauss_part = jax.random.normal(first, (TOKENS, KVH, HD), jnp.float32)
    row_scale = jnp.exp(jax.random.uniform(second, (TOKENS, 1, 1), jnp.float32, -0.7, 0.7))
    result = row_scale * gauss_part
    return jnp.clip(result, -8.0, 8.0).reshape(TOKENS, KVH * HD).astype(jnp.bfloat16)


def block_scale(own_key, shape, cuts, smallest, largest):
    def one(dim, blocks):
        draws = jax.random.uniform(jax.random.fold_in(jax.random.fold_in(own_key, 6), dim), (blocks,), jnp.float32, smallest / len(cuts), largest / len(cuts))
        return jnp.repeat(jnp.exp(draws), shape[dim] // blocks).reshape((-1,) + (1,) * (len(shape) - dim - 1))

    level = one(*cuts[0])
    for cut in cuts[1:]:
        level = level * one(*cut)
    return level


def length_profile(number_of, total, reach, lean):
    loads = [(1 << 20) // math.isqrt(grade ** lean) + 1 for grade in range(2, number_of + 1)]
    rest, holding = total - reach - (number_of - 1), [1] * (number_of - 1)
    while rest > 0:
        movable = [i for i in range(number_of - 1) if holding[i] < reach]
        mass, budget = sum([loads[i] for i in movable]), rest
        for i in movable:
            addition = min(reach - holding[i], max(1, budget * loads[i] // mass), rest)
            holding[i] = holding[i] + addition
            rest = rest - addition
    return np.array([reach] + holding)


def uneven(own_key, count, total, most, skew):
    if count == 2:
        one = jax.random.randint(own_key, (), max(1, total - most), min(most, total - 1) + 1)
        return jnp.stack([one, total - one])
    sizes = jnp.asarray(length_profile(count, total, most, skew), jnp.int32)
    couples = (count - 1) // 2
    donor, taker = sizes[1:1 + 2 * couples:2], sizes[2:2 + 2 * couples:2]
    room = jnp.minimum(donor - 1, most - taker)
    moved = jax.random.randint(jax.random.fold_in(own_key, 1), (couples,), 0, 1 << 20) % (room + 1)
    sizes = sizes.at[1:1 + 2 * couples:2].set(donor - moved).at[2:2 + 2 * couples:2].set(taker + moved)
    return sizes[jax.random.permutation(jax.random.fold_in(own_key, 2), count)]


def gaussian(rng, extent, width, most, pieces=(), kind=jnp.bfloat16):
    factor_of = block_scale(rng, extent, pieces, -0.22, 0.18) if pieces else 1.0
    entries = jax.random.normal(rng, extent, jnp.float32) * width * factor_of
    return jnp.minimum(jnp.maximum(entries, -most), most).astype(kind)


def setup_inputs(seed: int = 0) -> dict:
    arg_keys = jax.random.split(jax.random.key(seed), 6)
    return {
        "queries": draw_queries(jax.random.fold_in(arg_keys[5], 71), 0),
        "keys": draw_keys(jax.random.fold_in(arg_keys[5], 71), 0),
        "values": gaussian(arg_keys[2], (TOKENS, KW), 1.0, 6.0, ((0, 256),)),
        "slot_order": jax.vmap(lambda own: jax.random.permutation(own, TOK_DEV))(jax.random.split(arg_keys[3], N_GRP * N_SP)).reshape((N_GRP, N_SP, TOK_DEV)).astype(jnp.int32),
        "doc_ids": jax.vmap(lambda own: jnp.searchsorted(jnp.cumsum(uneven(own, DOCS, GROUP_TOK, MAXDOC, 2)), jnp.arange(GROUP_TOK), side="right"))(jax.random.split(arg_keys[4], N_GRP)).reshape((N_GRP, GROUP_TOK)).astype(jnp.int32),
    }


def to_group_layout(packed, slot_perm):
    shaped = packed.reshape(N_GRP, N_SP, TOK_DEV, packed.shape[-1])
    chosen = jnp.take_along_axis(shaped, slot_perm[..., None], axis=2)
    split_rows = chosen.reshape(N_GRP, N_SP, N_GRP, TOK_DEV // N_GRP, packed.shape[-1])
    return split_rows.transpose(2, 1, 0, 3, 4).reshape(N_GRP, N_SP, TOK_DEV, packed.shape[-1])


def from_group_layout(grouped, slot_perm):
    split_rows = grouped.reshape(N_GRP, N_SP, N_GRP, TOK_DEV // N_GRP, grouped.shape[-1])
    blocks = split_rows.transpose(2, 1, 0, 3, 4).reshape(N_GRP, N_SP, TOK_DEV, grouped.shape[-1])

    def place(perm_row, rows_in):
        return jnp.zeros_like(rows_in).at[perm_row].set(rows_in)

    placed = jax.vmap(jax.vmap(place))(slot_perm, blocks)
    return placed.reshape(TOKENS, grouped.shape[-1])


def window_mask(seg_padded, member, rows_dev, max_reach):
    key_seg = lax.dynamic_slice_in_dim(seg_padded, member * rows_dev, (max_reach + 1) * rows_dev)
    query_seg = lax.dynamic_slice_in_dim(seg_padded, (member + max_reach) * rows_dev, rows_dev)
    column = jnp.arange((max_reach + 1) * rows_dev, dtype=jnp.int32)
    row_pos = jnp.arange(rows_dev, dtype=jnp.int32)
    same_doc = key_seg[None, :] == query_seg[:, None]
    return same_doc & (column[None, :] <= row_pos[:, None] + max_reach * rows_dev)


def attention_rows(query_rows, key_win, val_win, allowed):
    scale = HD ** -0.5
    group_size = QH // KVH
    query_wide = query_rows.astype(jnp.float32).reshape(-1, KVH, group_size, HD)
    head_outputs = []
    for kv_head in range(KVH):
        key_head = key_win[:, kv_head * HD:(kv_head + 1) * HD].astype(jnp.float32)
        val_head = val_win[:, kv_head * HD:(kv_head + 1) * HD].astype(jnp.float32)
        scores = jnp.einsum("rgd,cd->grc", query_wide[:, kv_head], key_head) * scale
        scores = jnp.where(allowed[None], scores, -1e30)
        row_max = jnp.max(scores, axis=-1, keepdims=True)
        exponent = jnp.exp(scores - row_max)
        denominator = jnp.sum(exponent, axis=-1)
        weights = lax.optimization_barrier(exponent.astype(jnp.bfloat16)).astype(jnp.float32)
        mixed_out = jnp.einsum("grc,cd->rgd", weights, val_head) / denominator.T[:, :, None]
        head_outputs.append(mixed_out)
    return jnp.stack(head_outputs, axis=1).reshape(query_rows.shape[0], QH * HD).astype(jnp.bfloat16)


def reference(queries, keys, values, slot_order, doc_ids):
    group_q = to_group_layout(queries, slot_order)
    group_k = to_group_layout(keys, slot_order).reshape(N_GRP, GROUP_TOK, KW)
    group_v = to_group_layout(values, slot_order).reshape(N_GRP, GROUP_TOK, KW)
    zero_rows = jnp.zeros((N_GRP, SPAN * TOK_DEV, KW), jnp.bfloat16)
    keys_padded = jnp.concatenate([zero_rows, group_k], axis=1)
    vals_padded = jnp.concatenate([zero_rows, group_v], axis=1)
    seg_padded = jnp.concatenate([jnp.full((N_GRP, SPAN * TOK_DEV), -1, jnp.int32), doc_ids.astype(jnp.int32)], axis=1)

    def per_device(flat_index):
        group = flat_index // N_SP
        member = flat_index % N_SP
        query_rows = group_q[group, member]
        key_win = lax.dynamic_slice_in_dim(keys_padded[group], member * TOK_DEV, (SPAN + 1) * TOK_DEV, 0)
        val_win = lax.dynamic_slice_in_dim(vals_padded[group], member * TOK_DEV, (SPAN + 1) * TOK_DEV, 0)
        allowed = window_mask(seg_padded[group], member, TOK_DEV, SPAN)
        return attention_rows(query_rows, key_win, val_win, allowed)

    context = lax.map(per_device, jnp.arange(N_GRP * N_SP, dtype=jnp.int32))
    return from_group_layout(context.reshape(N_GRP, N_SP, TOK_DEV, QW), slot_order)
```

```python
import functools

import jax
import jax.numpy as jnp
from jax import lax
from jax.experimental import pallas as pl
from jax.experimental.pallas import tpu as pltpu
from jax.sharding import Mesh
from jax.sharding import PartitionSpec as P

QH = 40
KVH = 8
HD = 128
GS = QH // KVH
NZ = 8
NSY = 32
NG = 4
ROWS = 8
CHUNKS = 2
GC = NG // CHUNKS
TILE_SY = 4
TROWS = TILE_SY * ROWS
NT = NSY // TILE_SY
SPAN_POS = TILE_SY * 64
MAXB = 5
NEG = -1e30
PLANE = ("yh", "x", "c", "yl")
VMEM_LIMIT = 48 * 1024 * 1024


def one_hot_t(slot):
    rows = lax.broadcasted_iota(jnp.int32, (128, 128), 0)
    return (rows == slot).astype(jnp.float32).astype(jnp.bfloat16)


def pick(onehot, x):
    return lax.dot_general(
        onehot, x, (((0,), (0,)), ((), ())), preferred_element_type=jnp.float32
    ).astype(jnp.bfloat16)


def kv_send_kernel(slot_ref, k_ref, v_ref, o_ref):
    onehot = one_hot_t(slot_ref[...])
    for part, ref in enumerate((k_ref, v_ref)):
        got = pick(onehot, ref[...])
        for h in range(KVH):
            for yl in range(2):
                for yh in range(2):
                    at = (yl * 2 + yh) * 32
                    o_ref[yh, h, yl, :, part * HD : (part + 1) * HD] = got[
                        at : at + 32, h * HD : (h + 1) * HD
                    ]


def q_send_kernel(slot_ref, q_ref, o_ref):
    onehot = one_hot_t(slot_ref[...])
    for h in range(KVH):
        got = pick(onehot, q_ref[:, h * GS * HD : (h + 1) * GS * HD])
        for yl in range(2):
            for yh in range(2):
                at = (yl * 2 + yh) * 32
                o_ref[yh, h, yl] = got[at : at + 32]


def put_back_kernel(slot_ref, *refs):
    parts, o_ref = refs[:-1], refs[-1]
    onehot = one_hot_t(slot_ref[...])
    for h in range(KVH):
        rows = [p[yh, h, yl] for yl in range(2) for yh in range(2) for p in parts]
        got = jnp.dot(onehot, jnp.concatenate(rows, axis=0), preferred_element_type=jnp.float32)
        o_ref[:, h * GS * HD : (h + 1) * GS * HD] = got.astype(jnp.bfloat16)


def attention_kernel(first_gg, info_ref, bounds_ref, q_ref, *refs):
    kv_refs, o_ref = refs[:NZ], refs[NZ]
    gg = pl.program_id(0) + first_gg
    row = info_ref[NZ + 1] + gg
    b1, b2, b3 = bounds_ref[row, 0], bounds_ref[row, 1], bounds_ref[row, 2]
    z0 = info_ref[NZ]

    q_iota = lax.broadcasted_iota(jnp.int32, (TROWS, 1), 0)
    q_rel = (q_iota // 8) * 64 + q_iota % 8 + z0 * 8
    k_iota = lax.broadcasted_iota(jnp.int32, (1, NZ * TROWS), 1)
    k_z = jnp.zeros_like(k_iota)
    for i in range(NZ):
        k_z = jnp.where(k_iota // TROWS == i, info_ref[i], k_z)
    k_in = k_iota % TROWS
    k_rel = (k_in // 8) * 64 + k_in % 8 + k_z * 8
    log2e_scale = (HD**-0.5) * 1.4426950408889634

    def tile(t, carry):
        first_pos = t * SPAN_POS + z0 * 8
        first_start = jnp.where(
            first_pos >= b3, b3, jnp.where(first_pos >= b2, b2, jnp.where(first_pos >= b1, b1, 0))
        )
        low = first_start // SPAN_POS
        q_pos = t * SPAN_POS + q_rel
        q_start = jnp.where(
            q_pos >= b3, b3, jnp.where(q_pos >= b2, b2, jnp.where(q_pos >= b1, b1, 0))
        )
        row0 = pl.multiple_of(t * TROWS, TROWS)
        q_tile = q_ref[0, :, pl.ds(row0, TROWS), :].reshape(GS * TROWS, HD)

        def work(count):
            keys, vals, oks = [], [], []
            for n in range(count):
                b = t - (count - 1) + n
                k0 = pl.multiple_of(b * TROWS, TROWS)
                for r in kv_refs:
                    keys.append(r[0, pl.ds(k0, TROWS), :HD])
                    vals.append(r[0, pl.ds(k0, TROWS), HD:])
                k_pos = b * SPAN_POS + k_rel
                oks.append((k_pos <= q_pos) & (k_pos >= q_start))
            keys = jnp.concatenate(keys, axis=0)
            vals = jnp.concatenate(vals, axis=0)
            ok = jnp.concatenate(oks, axis=1)
            s = lax.dot_general(
                q_tile, keys, (((1,), (1,)), ((), ())), preferred_element_type=jnp.float32
            )
            s = s.reshape(GS, TROWS, count * SPAN_POS)
            s = jnp.where(ok[None], s, NEG)
            m = jnp.max(s, axis=-1, keepdims=True)
            p = jnp.exp2((s - m) * log2e_scale)
            total = jnp.sum(p, axis=-1, keepdims=True)
            w = p.astype(jnp.bfloat16).reshape(GS * TROWS, count * SPAN_POS)
            out = jnp.dot(w, vals, preferred_element_type=jnp.float32)
            out = out.reshape(GS, TROWS, HD) / total
            for hh in range(GS):
                for i in range(TILE_SY):
                    o_ref[t * TILE_SY + i, 0, :, hh * HD : (hh + 1) * HD] = out[
                        hh, i * 8 : (i + 1) * 8
                    ].astype(jnp.bfloat16)

        for count in range(1, MAXB + 1):
            pl.when(t - low + 1 == count)(functools.partial(work, count))
        return carry

    lax.fori_loop(0, NT, tile, 0)


def attention(chunk, info, bounds, q, kvs):
    first = chunk * GC
    smem = pl.BlockSpec(memory_space=pltpu.SMEM)
    return pl.pallas_call(
        functools.partial(attention_kernel, first),
        grid=(GC,),
        out_shape=jax.ShapeDtypeStruct((NSY, GC, ROWS, GS * HD), jnp.bfloat16),
        in_specs=[smem, smem, pl.BlockSpec((1, GS, NSY * ROWS, HD), lambda g: (g + first, 0, 0, 0))]
        + [pl.BlockSpec((1, NSY * ROWS, 2 * HD), lambda g: (g, 0, 0))] * NZ,
        out_specs=pl.BlockSpec((NSY, 1, ROWS, GS * HD), lambda g: (0, g, 0, 0)),
        compiler_params=pltpu.CompilerParams(vmem_limit_bytes=VMEM_LIMIT),
        cost_estimate=pl.CostEstimate(
            flops=800_000_000, bytes_accessed=4_000_000, transcendentals=2_000_000
        ),
        name="attention",
    )(info, bounds, q, *kvs)


def whole(kernel, out_shape, *args):
    return pl.pallas_call(
        kernel,
        out_shape=out_shape,
        compiler_params=pltpu.CompilerParams(vmem_limit_bytes=VMEM_LIMIT),
        name=kernel.__name__,
    )(*args)


def swap(value, axes):
    return lax.all_to_all(value, axes, split_axis=0, concat_axis=0, tiled=True)


def along_z(value, step):
    return lax.ppermute(value, "z", [(i, (i + step) % NZ) for i in range(NZ)])


def on_device(queries, keys, values, slot_order, doc_ids):
    slot = slot_order[0]
    bf16 = jnp.bfloat16
    z0 = lax.axis_index("z")

    kv_out = whole(
        kv_send_kernel, jax.ShapeDtypeStruct((2, KVH, 2, 32, 2 * HD), bf16), slot, keys, values
    )
    kv = swap(kv_out.reshape(NSY, 32, 2 * HD), PLANE)
    kv = kv.reshape(NSY, NG, ROWS, 2 * HD).transpose(1, 0, 2, 3).reshape(NG, NSY * ROWS, 2 * HD)

    q_out = whole(q_send_kernel, jax.ShapeDtypeStruct((2, KVH, 2, 32, GS * HD), bf16), slot, queries)
    q = swap(q_out.reshape(NSY, 32, GS * HD), PLANE)
    q = q.reshape(NSY, NG, ROWS, GS, HD).transpose(1, 3, 0, 2, 4).reshape(NG, GS, NSY * ROWS, HD)

    edges = jnp.sum(doc_ids[0][None, :] < jnp.arange(1, 4, dtype=jnp.int32)[:, None], axis=1)
    edges = jnp.zeros((128,), jnp.int32).at[:3].set(edges.astype(jnp.int32))
    bounds = swap(jnp.broadcast_to(edges[None, None], (NZ, 8, 128)).reshape(NZ * 8, 128), ("z",))
    bounds = bounds.reshape(NZ, 8, 128)[:, 0]

    up = [kv[c * GC : (c + 1) * GC] for c in range(CHUNKS)]
    down = list(up)
    have = [[part] for part in up]
    for step in range(NZ // 2 - 1):
        for c in range(CHUNKS):
            up[c] = along_z(up[c], 1)
            down[c] = along_z(down[c], -1)
            have[c] += [up[c], down[c]]
    for c in range(CHUNKS):
        have[c].append(along_z(up[c], 1) if c % 2 == 0 else along_z(down[c], -1))
    offsets = [0, -1, 1, -2, 2, -3, 3, 4]
    info = jnp.stack([(z0 + o + NZ) % NZ for o in offsets] + [z0, lax.axis_index("yh") * NG])
    info = info.astype(jnp.int32)

    back = []
    for c in range(CHUNKS):
        out = attention(c, info, bounds, q, have[c])
        got = swap(out.reshape(NSY, GC * ROWS, GS * HD), PLANE)
        back.append(got.reshape(2, KVH, 2, GC * ROWS, GS * HD))
    return whole(
        put_back_kernel, jax.ShapeDtypeStruct((128, QH * HD), bf16), slot, *back
    )


def solution(mesh):
    fine = Mesh(mesh.devices.reshape(2, NZ, 2, 4, 2), ("yl", "z", "yh", "x", "c"))
    rows = P(("yl", "z", "yh", "x", "c"), None)
    return jax.shard_map(
        on_device,
        mesh=fine,
        in_specs=(rows, rows, rows, P(("yl", "z"), ("yh", "x", "c"), None), P(("yl", "z"), None)),
        out_specs=rows,
        check_vma=False,
    )
```

```python
import functools

import jax
import jax.numpy as jnp
from jax import lax
from jax.experimental import pallas as pl
from jax.experimental.pallas import tpu as pltpu
from jax.sharding import Mesh
from jax.sharding import PartitionSpec as P

QH = 40
KVH = 8
HD = 128
GS = QH // KVH
NZ = 8
NSY = 32
NG = 4
ROWS = 8
KROWS = NSY * ROWS
CHUNKS = 2
GC = NG // CHUNKS
TILE_SY = 8
TROWS = TILE_SY * ROWS
NT = NSY // TILE_SY
TILE_POS = TILE_SY * 64
BLOCK_POS = 256
BLOCK_ROWS = BLOCK_POS // NZ
TILE_BLOCKS = TILE_POS // BLOCK_POS
MAXB = TILE_BLOCKS + 4
NEG = -1e30
PLANE = ("yh", "x", "c", "yl")


def one_hot_t(slot):
    rows = lax.broadcasted_iota(jnp.int32, (128, 128), 0)
    return (rows == slot).astype(jnp.float32).astype(jnp.bfloat16)


def pick(onehot, x):
    return lax.dot_general(
        onehot, x, (((0,), (0,)), ((), ())), preferred_element_type=jnp.float32
    ).astype(jnp.bfloat16)


def kv_send_kernel(slot_ref, k_ref, v_ref, o_ref):
    onehot = one_hot_t(slot_ref[...])
    for part, ref in enumerate((k_ref, v_ref)):
        got = pick(onehot, ref[...])
        for h in range(KVH):
            for yl in range(2):
                for yh in range(2):
                    at = (yl * 2 + yh) * 32
                    o_ref[yh, h, yl, :, part * HD : (part + 1) * HD] = got[
                        at : at + 32, h * HD : (h + 1) * HD
                    ]


def ring_kernel(kv_ref, doc_ref, *o_refs):
    doc = doc_ref[...]
    lane = lax.broadcasted_iota(jnp.int32, (16, 2 * HD), 1)
    extra = jnp.zeros((16, 2 * HD), jnp.float32)
    for i in range(3):
        edge = jnp.sum((doc <= i).astype(jnp.int32), axis=1, keepdims=True)
        extra = jnp.where(lane == 2 * i, (edge // 64).astype(jnp.float32), extra)
        extra = jnp.where(lane == 2 * i + 1, (edge % 64).astype(jnp.float32), extra)
    rows = [kv_ref[sy].astype(jnp.float32) for sy in range(NSY)]
    for c, o_ref in enumerate(o_refs):
        for g in range(GC):
            at = (c * GC + g) * ROWS
            part = jnp.concatenate([r[at : at + ROWS] for r in rows], axis=0)
            o_ref[g * KROWS : (g + 1) * KROWS, :] = part.astype(jnp.bfloat16)
        o_ref[GC * KROWS :, :] = extra.astype(jnp.bfloat16)


def q_send_kernel(slot_ref, q_ref, o_ref):
    onehot = one_hot_t(slot_ref[...])
    for h in range(KVH):
        got = pick(onehot, q_ref[:, h * GS * HD : (h + 1) * GS * HD])
        for yl in range(2):
            for yh in range(2):
                at = (yl * 2 + yh) * 32
                o_ref[yh, h, yl] = got[at : at + 32]


def put_back_kernel(slot_ref, *refs):
    parts, o_ref = refs[:-1], refs[-1]
    onehot = one_hot_t(slot_ref[...])
    for h in range(KVH):
        rows = [p[yh, h, yl] for yl in range(2) for yh in range(2) for p in parts]
        got = jnp.dot(onehot, jnp.concatenate(rows, axis=0), preferred_element_type=jnp.float32)
        o_ref[:, h * GS * HD : (h + 1) * GS * HD] = got.astype(jnp.bfloat16)


def doc_start(pos, inner):
    b1, b2, b3 = inner
    return jnp.where(pos >= b3, b3, jnp.where(pos >= b2, b2, jnp.where(pos >= b1, b1, 0)))


def attention_kernel(info_ref, q_ref, *refs):
    kv_refs, o_ref = [refs[c * NZ : (c + 1) * NZ] for c in range(CHUNKS)], refs[-1]
    z0 = info_ref[NZ]
    q_iota = lax.broadcasted_iota(jnp.int32, (TROWS, 1), 0)
    q_rel = (q_iota // 8) * 64 + q_iota % 8 + z0 * 8
    k_iota = lax.broadcasted_iota(jnp.int32, (1, BLOCK_POS), 1)
    k_z = jnp.zeros_like(k_iota)
    for i in range(NZ):
        k_z = jnp.where(k_iota // BLOCK_ROWS == i, info_ref[i], k_z)
    k_in = k_iota % BLOCK_ROWS
    k_rel = (k_in // 8) * 64 + k_in % 8 + k_z * 8
    scale = (HD**-0.5) * 1.4426950408889634
    extras = [r[GC * KROWS :, :HD].astype(jnp.float32) for r in kv_refs[0]]
    inner = []
    for gg in range(NG):
        mine = jnp.zeros_like(extras[0])
        for i in range(NZ):
            mine = jnp.where(info_ref[i] == info_ref[NZ + 1] + gg, extras[i], mine)
        found = [mine[0, lane].astype(jnp.int32) for lane in range(6)]
        inner.append([found[2 * i] * 64 + found[2 * i + 1] for i in range(3)])

    def tile(t, carry):
        first_pos = t * TILE_POS + z0 * 8
        low = doc_start(first_pos, inner[0])
        for g in range(1, NG):
            low = jnp.minimum(low, doc_start(first_pos, inner[g]))
        low = low // BLOCK_POS
        top = (t + 1) * TILE_BLOCKS - 1
        q_pos = t * TILE_POS + q_rel
        row0 = pl.multiple_of(t * TROWS, TROWS)

        def work(count):
            for g in range(NG):
                q_start = doc_start(q_pos, inner[g])
                q_tile = q_ref[g, :, pl.ds(row0, TROWS), :].reshape(GS * TROWS, HD)
                keys, vals, oks = [], [], []
                for n in range(count):
                    block = top - (count - 1) + n
                    k0 = pl.multiple_of(g % GC * KROWS + block * BLOCK_ROWS, BLOCK_ROWS)
                    for r in kv_refs[g // GC]:
                        keys.append(r[pl.ds(k0, BLOCK_ROWS), :HD])
                        vals.append(r[pl.ds(k0, BLOCK_ROWS), HD:])
                    k_pos = block * BLOCK_POS + k_rel
                    oks.append((k_pos <= q_pos) & (k_pos >= q_start))
                keys = jnp.concatenate(keys, axis=0)
                vals = jnp.concatenate(vals, axis=0)
                vals = jnp.concatenate([vals, jnp.ones_like(vals)], axis=1)
                ok = jnp.concatenate(oks, axis=1)
                s = lax.dot_general(
                    q_tile, keys, (((1,), (1,)), ((), ())), preferred_element_type=jnp.float32
                )
                s = s.reshape(GS, TROWS, count * BLOCK_POS)
                s = jnp.where(ok[None], s, NEG)
                m = jnp.max(s, axis=-1, keepdims=True)
                p = jnp.exp2((s - m) * scale)
                w = p.astype(jnp.bfloat16).reshape(GS * TROWS, count * BLOCK_POS)
                out = jnp.dot(w, vals, preferred_element_type=jnp.float32)
                out = (out[:, :HD] / out[:, HD:]).reshape(GS, TROWS, HD)
                for hh in range(GS):
                    for i in range(TILE_SY):
                        o_ref[t * TILE_SY + i, g, :, hh * HD : (hh + 1) * HD] = out[
                            hh, i * 8 : (i + 1) * 8
                        ].astype(jnp.bfloat16)

        for count in range(TILE_BLOCKS, MAXB + 1):
            pl.when(top - low + 1 == count)(functools.partial(work, count))
        return carry

    lax.fori_loop(0, NT, tile, 0)


def attention(info, q, kvs):
    smem = pl.BlockSpec(memory_space=pltpu.SMEM)
    vmem = pl.BlockSpec(memory_space=pltpu.VMEM)
    return pl.pallas_call(
        attention_kernel,
        out_shape=jax.ShapeDtypeStruct((NSY, NG, ROWS, GS * HD), jnp.bfloat16),
        in_specs=[smem] + [vmem] * (1 + len(kvs)),
        out_specs=vmem,
        compiler_params=pltpu.CompilerParams(vmem_limit_bytes=24 * 1024 * 1024),
        cost_estimate=pl.CostEstimate(
            flops=1_600_000_000, bytes_accessed=7_000_000, transcendentals=4_000_000
        ),
        name="attention",
    )(info, q, *kvs)


def whole(kernel, mib, out_shape, *args):
    return pl.pallas_call(
        kernel,
        out_shape=out_shape,
        compiler_params=pltpu.CompilerParams(vmem_limit_bytes=mib * 1024 * 1024),
        name=kernel.__name__,
    )(*args)


def swap(value, axes):
    return lax.all_to_all(value, axes, split_axis=0, concat_axis=0, tiled=True)


def along_z(value, step):
    return lax.ppermute(value, "z", [(i, (i + step) % NZ) for i in range(NZ)])


def on_device(queries, keys, values, slot_order, doc_ids):
    slot = slot_order[0]
    bf16 = jnp.bfloat16
    z0 = lax.axis_index("z")

    kv_out = whole(
        kv_send_kernel, 60, jax.ShapeDtypeStruct((2, KVH, 2, 32, 2 * HD), bf16), slot, keys, values
    )
    q_out = whole(q_send_kernel, 24, jax.ShapeDtypeStruct((2, KVH, 2, 32, GS * HD), bf16), slot, queries)
    kv = swap(kv_out.reshape(NSY, 32, 2 * HD), PLANE)
    part = jax.ShapeDtypeStruct((GC * KROWS + 16, 2 * HD), bf16)
    up = list(whole(ring_kernel, 24, (part,) * CHUNKS, kv, doc_ids))
    down = list(up)
    have = [[one] for one in up]
    for step in range(NZ // 2 - 1):
        for c in range(CHUNKS):
            up[c] = along_z(up[c], 1)
            down[c] = along_z(down[c], -1)
            have[c] += [up[c], down[c]]
    for c in range(CHUNKS):
        have[c].append(along_z(up[c], 1) if c % 2 == 0 else along_z(down[c], -1))

    _, q_out = lax.optimization_barrier((have[0][0], q_out))
    q = swap(q_out.reshape(NSY, 32, GS * HD), PLANE)
    q = q.reshape(NSY, NG, ROWS, GS, HD).transpose(1, 3, 0, 2, 4).reshape(NG, GS, KROWS, HD)

    offsets = [0, -1, 1, -2, 2, -3, 3, 4]
    places = [(z0 + o + NZ) % NZ for o in offsets]
    info = jnp.stack(places + [z0, lax.axis_index("yh") * NG]).astype(jnp.int32)
    out = attention(info, q, [one for row in have for one in row])
    got = swap(out.reshape(NSY, NG * ROWS, GS * HD), PLANE)
    got = got.reshape(2, KVH, 2, NG * ROWS, GS * HD)
    return whole(
        put_back_kernel, 24, jax.ShapeDtypeStruct((128, QH * HD), bf16), slot, got
    )


def solution(mesh):
    fine = Mesh(mesh.devices.reshape(2, NZ, 2, 4, 2), ("yl", "z", "yh", "x", "c"))
    rows = P(("yl", "z", "yh", "x", "c"), None)
    return jax.shard_map(
        on_device,
        mesh=fine,
        in_specs=(rows, rows, rows, P(("yl", "z"), ("yh", "x", "c"), None), P(("yl", "z"), None)),
        out_specs=rows,
        check_vma=False,
    )
```

```python
import functools

import jax
import jax.numpy as jnp
from jax import lax
from jax.experimental import pallas as pl
from jax.experimental.pallas import tpu as pltpu
from jax.sharding import Mesh
from jax.sharding import PartitionSpec as P

QH = 40
KVH = 8
HD = 128
GS = QH // KVH
NZ = 8
NSY = 32
NG = 4
ROWS = 8
KROWS = NSY * ROWS
CHUNKS = 2
GC = NG // CHUNKS
TILE_SY = 4
JOIN = 2
TROWS = TILE_SY * ROWS
NT = NSY // TILE_SY
TILE_POS = TILE_SY * 64
BLOCK_POS = 256
BLOCK_ROWS = BLOCK_POS // NZ
TILE_BLOCKS = TILE_POS // BLOCK_POS
MAXB = TILE_BLOCKS + 4
NEG = -1e30
SCALE = (HD**-0.5) * 1.4426950408889634
PLANE = ("yh", "x", "c", "yl")


def one_hot_t(slot):
    rows = lax.broadcasted_iota(jnp.int32, (128, 128), 0)
    return (rows == slot).astype(jnp.float32).astype(jnp.bfloat16)


def pick(onehot, x):
    return lax.dot_general(
        onehot, x, (((0,), (0,)), ((), ())), preferred_element_type=jnp.float32
    ).astype(jnp.bfloat16)


def kv_send_kernel(slot_ref, k_ref, v_ref, o_ref):
    onehot = one_hot_t(slot_ref[...])
    for part, ref in enumerate((k_ref, v_ref)):
        got = pick(onehot, ref[...])
        for h in range(KVH):
            for yl in range(2):
                for yh in range(2):
                    at = (yl * 2 + yh) * 32
                    o_ref[yh, h, yl, :, part * HD : (part + 1) * HD] = got[
                        at : at + 32, h * HD : (h + 1) * HD
                    ]


def edge_kernel(doc_ref, o_ref):
    doc = doc_ref[...]
    lane = lax.broadcasted_iota(jnp.int32, (16, HD), 1)
    out = jnp.zeros((16, HD), jnp.float32)
    for i in range(3):
        edge = jnp.sum((doc <= i).astype(jnp.int32), axis=1, keepdims=True)
        out = jnp.where(lane == 2 * i, (edge // 64).astype(jnp.float32), out)
        out = jnp.where(lane == 2 * i + 1, (edge % 64).astype(jnp.float32), out)
    o_ref[...] = out.astype(jnp.bfloat16)


def ring_kernel(kv_ref, edge_ref, far_ref, *o_refs):
    rows = [kv_ref[sy].astype(jnp.float32) for sy in range(NSY)]
    for c, o_ref in enumerate(o_refs):
        for g in range(GC):
            at = (c * GC + g) * ROWS
            part = jnp.concatenate([r[at : at + ROWS] for r in rows], axis=0)
            o_ref[g * KROWS : (g + 1) * KROWS, :] = part.astype(jnp.bfloat16)
        o_ref[GC * KROWS :, :HD] = edge_ref[...]
        o_ref[GC * KROWS :, HD:] = far_ref[...]


def q_send_kernel(slot_ref, q_ref, o_ref):
    onehot = one_hot_t(slot_ref[...])
    for h in range(KVH):
        got = pick(onehot, q_ref[:, h * GS * HD : (h + 1) * GS * HD])
        for yl in range(2):
            for yh in range(2):
                at = (yl * 2 + yh) * 32
                o_ref[yh, h, yl] = got[at : at + 32]


def put_back_kernel(slot_ref, got_ref, o_ref, buf, sems):
    onehot = one_hot_t(slot_ref[...])
    stores = []
    for h in range(KVH):
        cols = pl.ds(h * GS * HD, GS * HD)
        rows = [got_ref[yh, h, yl] for yl in range(2) for yh in range(2)]
        back = jnp.dot(onehot, jnp.concatenate(rows, axis=0), preferred_element_type=jnp.float32)
        buf[:, cols] = back.astype(jnp.bfloat16)
        stores.append(pltpu.make_async_copy(buf.at[:, cols], o_ref.at[:, cols], sems.at[h]))
        stores[-1].start()
    for store in stores:
        store.wait()


def doc_start(pos, inner):
    b1, b2, b3 = inner
    return jnp.where(pos >= b3, b3, jnp.where(pos >= b2, b2, jnp.where(pos >= b1, b1, 0)))


def edges_of(info_ref, refs):
    tails = [r[GC * KROWS :, :HD].astype(jnp.float32) for r in refs[: NZ - 1]]
    tails.append(refs[0][GC * KROWS :, HD:].astype(jnp.float32))
    inner = []
    for gg in range(NG):
        mine = jnp.zeros_like(tails[0])
        for i in range(NZ):
            mine = jnp.where(info_ref[i] == info_ref[NZ + 1] + gg, tails[i], mine)
        found = [mine[0, lane].astype(jnp.int32) for lane in range(6)]
        inner.append([found[2 * i] * 64 + found[2 * i + 1] for i in range(3)])
    return inner


def near_kernel(chunk, info_ref, edge_in, q_ref, *refs):
    per = NZ - 1
    kv_refs = refs[:per]
    m_ref, acc_ref = refs[per : per + 2]
    z0 = info_ref[NZ]
    q_iota = lax.broadcasted_iota(jnp.int32, (TROWS, 1), 0)
    q_rel = (q_iota // 8) * 64 + q_iota % 8 + z0 * 8
    if chunk == 0:
        every = edges_of(info_ref, kv_refs)
        for g in range(NG):
            for i in range(3):
                refs[per + 2][g, i] = every[g][i]
    else:
        every = [[edge_in[g, i] for i in range(3)] for g in range(NG)]
    inner = every[chunk * GC : (chunk + 1) * GC]

    def tiles(u, carry):
        count_of = None
        for j in range(JOIN):
            t = u * JOIN + j
            first_pos = t * TILE_POS + z0 * 8
            for g in range(GC):
                low = doc_start(first_pos, inner[g]) // BLOCK_POS
                need = (t + 1) * TILE_BLOCKS - low
                count_of = need if count_of is None else jnp.maximum(count_of, need)

        def work(count):
            rows = count * BLOCK_ROWS
            width = -(-per * rows // 128) * 128
            col = lax.broadcasted_iota(jnp.int32, (1, width), 1)
            inside, k_z = col, jnp.full_like(col, info_ref[0])
            for i in range(1, per):
                inside = jnp.where(col >= i * rows, col - i * rows, inside)
                k_z = jnp.where(col >= i * rows, info_ref[i], k_z)
            k_rel = (inside // 8) * 64 + inside % 8 + k_z * 8
            k_rel = jnp.where(col >= per * rows, 1 << 20, k_rel)
            pad = [jnp.zeros((width - per * rows, HD), jnp.bfloat16)] * (width > per * rows)
            items, scores, vals = [], [], []
            for j in range(JOIN):
                t = u * JOIN + j
                row0 = pl.multiple_of(t * TROWS, TROWS)
                block = jnp.maximum((t + 1) * TILE_BLOCKS - count, 0)
                for g in range(GC):
                    q_tile = q_ref[chunk * GC + g, :, pl.ds(row0, TROWS), :]
                    k0 = pl.multiple_of(g * KROWS + block * BLOCK_ROWS, BLOCK_ROWS)
                    at = pl.ds(k0, rows)
                    keys = jnp.concatenate([r[at, :HD] for r in kv_refs] + pad, axis=0)
                    val = jnp.concatenate([r[at, HD:] for r in kv_refs] + pad, axis=0)
                    vals.append(jnp.concatenate([val, jnp.ones_like(val)], axis=1))
                    s = lax.dot_general(
                        q_tile.reshape(GS * TROWS, HD),
                        keys,
                        (((1,), (1,)), ((), ())),
                        preferred_element_type=jnp.float32,
                    )
                    k_pos = block * BLOCK_POS + k_rel
                    q_pos = t * TILE_POS + q_rel
                    ok = (k_pos <= q_pos) & (k_pos >= doc_start(q_pos, inner[g]))
                    bias = jnp.where(ok, 0.0, NEG)
                    scores.append(s.reshape(GS, TROWS, width) + bias[None])
                    items.append((g, row0))
            tops = [jnp.max(s, axis=-1, keepdims=True) for s in scores]
            weights = [
                jnp.exp2((s - m) * SCALE).astype(jnp.bfloat16).reshape(GS * TROWS, width)
                for s, m in zip(scores, tops)
            ]
            outs = [
                jnp.dot(w, v, preferred_element_type=jnp.float32) for w, v in zip(weights, vals)
            ]
            for (g, row0), top, out in zip(items, tops, outs):
                at = pl.ds(row0, TROWS)
                acc_ref[g, :, at, :] = out.reshape(GS, TROWS, 2 * HD)
                m_ref[g, :, at, :] = jnp.broadcast_to(top, (GS, TROWS, HD))

        for count in range(TILE_BLOCKS, MAXB + 1):
            pl.when(count_of == count)(functools.partial(work, count))
        return carry

    lax.fori_loop(0, NT // JOIN, tiles, 0)


def far_kernel(info_ref, edge_ref, q_ref, *refs):
    m_refs, acc_refs, kv_refs = (refs[i * CHUNKS : (i + 1) * CHUNKS] for i in range(3))
    o_ref = refs[3 * CHUNKS]
    r_iota = lax.broadcasted_iota(jnp.int32, (KROWS, 1), 0)
    c_iota = lax.broadcasted_iota(jnp.int32, (1, KROWS), 1)
    q_pos = (r_iota // 8) * 64 + r_iota % 8 + info_ref[NZ] * 8
    k_pos = (c_iota // 8) * 64 + c_iota % 8 + info_ref[NZ - 1] * 8
    for g in range(NG):
        q_start = doc_start(q_pos, [edge_ref[g, i] for i in range(3)])
        bias = jnp.where((k_pos <= q_pos) & (k_pos >= q_start), 0.0, NEG)
        at = pl.ds(g % GC * KROWS, KROWS)
        keys, val = kv_refs[g // GC][at, :HD], kv_refs[g // GC][at, HD:]
        val = jnp.concatenate([val, jnp.ones_like(val)], axis=1)
        for hh in range(GS):
            s = lax.dot_general(
                q_ref[g, hh], keys, (((1,), (1,)), ((), ())), preferred_element_type=jnp.float32
            )
            s = s + bias
            before = m_refs[g // GC][g % GC, hh]
            m = jnp.maximum(before, jnp.max(s, axis=-1, keepdims=True))
            w = jnp.exp2((s - jnp.concatenate([m, m], axis=1)) * SCALE).astype(jnp.bfloat16)
            out = jnp.dot(w, val, preferred_element_type=jnp.float32)
            fade = jnp.exp2((before - m) * SCALE)
            acc = acc_refs[g // GC][g % GC, hh]
            num = acc[:, :HD] * fade + out[:, :HD]
            den = acc[:, HD:] * fade + out[:, HD:]
            o_ref[:, g, :, hh * HD : (hh + 1) * HD] = (
                (num / den).reshape(NSY, ROWS, HD).astype(jnp.bfloat16)
            )


def attention_near(chunk, info, edges, q, kvs):
    smem = pl.BlockSpec(memory_space=pltpu.SMEM)
    vmem = pl.BlockSpec(memory_space=pltpu.VMEM)
    out_shape = [
        jax.ShapeDtypeStruct((GC, GS, KROWS, HD), jnp.float32),
        jax.ShapeDtypeStruct((GC, GS, KROWS, 2 * HD), jnp.float32),
    ]
    out_specs = [vmem, vmem]
    if chunk == 0:
        out_shape.append(jax.ShapeDtypeStruct((NG, 3), jnp.int32))
        out_specs.append(smem)
    return pl.pallas_call(
        functools.partial(near_kernel, chunk),
        out_shape=out_shape,
        in_specs=[smem, smem] + [vmem] * (1 + len(kvs)),
        out_specs=out_specs,
        compiler_params=pltpu.CompilerParams(vmem_limit_bytes=24 * 1024 * 1024),
        cost_estimate=pl.CostEstimate(
            flops=800_000_000, bytes_accessed=10_000_000, transcendentals=2_000_000
        ),
        name="attention_near",
    )(info, edges, q, *kvs)


def attention_far(info, edges, q, *kvs):
    smem = pl.BlockSpec(memory_space=pltpu.SMEM)
    vmem = pl.BlockSpec(memory_space=pltpu.VMEM)
    return pl.pallas_call(
        far_kernel,
        out_shape=jax.ShapeDtypeStruct((NSY, NG, ROWS, GS * HD), jnp.bfloat16),
        in_specs=[smem, smem] + [vmem] * (1 + len(kvs)),
        out_specs=vmem,
        compiler_params=pltpu.CompilerParams(vmem_limit_bytes=24 * 1024 * 1024),
        cost_estimate=pl.CostEstimate(
            flops=800_000_000, bytes_accessed=7_000_000, transcendentals=1_500_000
        ),
        name="attention_far",
    )(info, edges, q, *kvs)


def whole(kernel, mib, out_shape, *args):
    return pl.pallas_call(
        kernel,
        out_shape=out_shape,
        compiler_params=pltpu.CompilerParams(vmem_limit_bytes=mib * 1024 * 1024),
        name=kernel.__name__,
    )(*args)


def swap(value, axes):
    return lax.all_to_all(value, axes, split_axis=0, concat_axis=0, tiled=True)


def along_z(value, step):
    return lax.ppermute(value, "z", [(i, (i + step) % NZ) for i in range(NZ)])


def on_device(queries, keys, values, slot_order, doc_ids):
    slot = slot_order[0]
    bf16 = jnp.bfloat16
    z0 = lax.axis_index("z")

    kv_out = whole(
        kv_send_kernel, 60, jax.ShapeDtypeStruct((2, KVH, 2, 32, 2 * HD), bf16), slot, keys, values
    )
    q_out = whole(q_send_kernel, 24, jax.ShapeDtypeStruct((2, KVH, 2, 32, GS * HD), bf16), slot, queries)
    kv = swap(kv_out.reshape(NSY, 32, 2 * HD), PLANE)
    _, doc_ids = lax.optimization_barrier((kv_out, doc_ids))
    edge = whole(edge_kernel, 24, jax.ShapeDtypeStruct((16, HD), bf16), doc_ids)
    part = jax.ShapeDtypeStruct((GC * KROWS + 16, 2 * HD), bf16)
    up = list(whole(ring_kernel, 24, (part,) * CHUNKS, kv, edge, along_z(edge, NZ // 2)))
    down = list(up)
    have = [[one] for one in up]
    for step in range(NZ // 2 - 1):
        for c in range(CHUNKS):
            up[c] = along_z(up[c], 1)
            down[c] = along_z(down[c], -1)
            have[c] += [up[c], down[c]]
    _, q_out = lax.optimization_barrier((have[0][0], q_out))
    q = swap(q_out.reshape(NSY, 32, GS * HD), PLANE)
    q = q.reshape(NSY, NG, ROWS, GS, HD).transpose(1, 3, 0, 2, 4).reshape(NG, GS, KROWS, HD)

    offsets = [0, -1, 1, -2, 2, -3, 3, 4]
    places = [(z0 + o + NZ) % NZ for o in offsets]
    info = jnp.stack(places + [z0, lax.axis_index("yh") * NG]).astype(jnp.int32)
    last = [along_z(up[0], 1), along_z(down[1], -1)]
    m0, acc0, edges = attention_near(0, info, info[None], q, have[0])
    m1, acc1 = attention_near(1, info, edges, q, have[1])
    out = attention_far(info, edges, q, m0, m1, acc0, acc1, *last)
    got = swap(out.reshape(NSY, NG * ROWS, GS * HD), PLANE)
    got = got.reshape(2, KVH, 2, NG * ROWS, GS * HD)
    vmem = pl.BlockSpec(memory_space=pltpu.VMEM)
    return pl.pallas_call(
        put_back_kernel,
        out_shape=jax.ShapeDtypeStruct((128, QH * HD), bf16),
        in_specs=[vmem, vmem],
        out_specs=pl.BlockSpec(memory_space=pltpu.HBM),
        scratch_shapes=[pltpu.VMEM((128, QH * HD), bf16), pltpu.SemaphoreType.DMA((KVH,))],
        compiler_params=pltpu.CompilerParams(vmem_limit_bytes=24 * 1024 * 1024),
        name="put_back",
    )(slot, got)


def solution(mesh):
    fine = Mesh(mesh.devices.reshape(2, NZ, 2, 4, 2), ("yl", "z", "yh", "x", "c"))
    rows = P(("yl", "z", "yh", "x", "c"), None)
    return jax.shard_map(
        on_device,
        mesh=fine,
        in_specs=(rows, rows, rows, P(("yl", "z"), ("yh", "x", "c"), None), P(("yl", "z"), None)),
        out_specs=rows,
        check_vma=False,
    )
```

```python
import functools

import jax
import jax.numpy as jnp
from jax import lax
from jax.experimental import pallas as pl
from jax.experimental.pallas import tpu as pltpu
from jax.sharding import Mesh
from jax.sharding import PartitionSpec as P

QH = 40
KVH = 8
HD = 128
GS = QH // KVH
NZ = 8
NSY = 32
NG = 4
ROWS = 8
KROWS = NSY * ROWS
CHUNKS = 2
GC = NG // CHUNKS
TILE_SY = 4
JOIN = 2
TROWS = TILE_SY * ROWS
NT = NSY // TILE_SY
TILE_POS = TILE_SY * 64
BLOCK_POS = 256
BLOCK_ROWS = BLOCK_POS // NZ
TILE_BLOCKS = TILE_POS // BLOCK_POS
MAXB = TILE_BLOCKS + 4
NEG = -1e30
SCALE = (HD**-0.5) * 1.4426950408889634
PLANE = ("yh", "x", "c", "yl")


def one_hot_t(slot):
    rows = lax.broadcasted_iota(jnp.int32, (128, 128), 0)
    return (rows == slot).astype(jnp.float32).astype(jnp.bfloat16)


def pick(onehot, x):
    return lax.dot_general(
        onehot, x, (((0,), (0,)), ((), ())), preferred_element_type=jnp.float32
    ).astype(jnp.bfloat16)


def kv_send_kernel(slot_ref, k_ref, v_ref, o_ref, buf, sems):
    loads = [
        pltpu.make_async_copy(ref, buf.at[i], sems.at[i]) for i, ref in enumerate((k_ref, v_ref))
    ]
    for load in loads:
        load.start()
    onehot = one_hot_t(slot_ref[...])
    for part in range(2):
        loads[part].wait()
        got = pick(onehot, buf[part])
        for h in range(KVH):
            for yl in range(2):
                for yh in range(2):
                    at = (yl * 2 + yh) * 32
                    o_ref[yh, h, yl, :, part * HD : (part + 1) * HD] = got[
                        at : at + 32, h * HD : (h + 1) * HD
                    ]


def edge_kernel(doc_ref, o_ref):
    doc = doc_ref[...]
    lane = lax.broadcasted_iota(jnp.int32, (16, HD), 1)
    out = jnp.zeros((16, HD), jnp.float32)
    for i in range(3):
        edge = jnp.sum((doc <= i).astype(jnp.int32), axis=1, keepdims=True)
        out = jnp.where(lane == 2 * i, (edge // 64).astype(jnp.float32), out)
        out = jnp.where(lane == 2 * i + 1, (edge % 64).astype(jnp.float32), out)
    o_ref[...] = out.astype(jnp.bfloat16)


def ring_kernel(kv_ref, edge_ref, far_ref, *o_refs):
    rows = [kv_ref[sy].astype(jnp.float32) for sy in range(NSY)]
    for c, o_ref in enumerate(o_refs):
        for g in range(GC):
            at = (c * GC + g) * ROWS
            part = jnp.concatenate([r[at : at + ROWS] for r in rows], axis=0)
            o_ref[g * KROWS : (g + 1) * KROWS, :] = part.astype(jnp.bfloat16)
        o_ref[GC * KROWS :, :HD] = edge_ref[...]
        o_ref[GC * KROWS :, HD:] = far_ref[...]


def q_send_kernel(slot_ref, q_ref, o_ref):
    onehot = one_hot_t(slot_ref[...])
    for h in range(KVH):
        got = pick(onehot, q_ref[:, h * GS * HD : (h + 1) * GS * HD])
        for yl in range(2):
            for yh in range(2):
                at = (yl * 2 + yh) * 32
                o_ref[yh, h, yl] = got[at : at + 32]


def put_back_kernel(slot_ref, got_ref, o_ref, buf, sems):
    onehot = one_hot_t(slot_ref[...])
    stores = []
    for h in range(KVH):
        cols = pl.ds(h * GS * HD, GS * HD)
        rows = [got_ref[yh, h, yl] for yl in range(2) for yh in range(2)]
        back = jnp.dot(onehot, jnp.concatenate(rows, axis=0), preferred_element_type=jnp.float32)
        buf[:, cols] = back.astype(jnp.bfloat16)
        stores.append(pltpu.make_async_copy(buf.at[:, cols], o_ref.at[:, cols], sems.at[h]))
        stores[-1].start()
    for store in stores:
        store.wait()


def doc_start(pos, inner):
    b1, b2, b3 = inner
    return jnp.where(pos >= b3, b3, jnp.where(pos >= b2, b2, jnp.where(pos >= b1, b1, 0)))


def edges_of(info_ref, refs):
    tails = [r[GC * KROWS :, :HD].astype(jnp.float32) for r in refs[: NZ - 1]]
    tails.append(refs[0][GC * KROWS :, HD:].astype(jnp.float32))
    inner = []
    for gg in range(NG):
        mine = jnp.zeros_like(tails[0])
        for i in range(NZ):
            mine = jnp.where(info_ref[i] == info_ref[NZ + 1] + gg, tails[i], mine)
        found = [mine[0, lane].astype(jnp.int32) for lane in range(6)]
        inner.append([found[2 * i] * 64 + found[2 * i + 1] for i in range(3)])
    return inner


def near_kernel(chunk, info_ref, edge_in, q_ref, *refs):
    per = NZ - 1
    kv_refs = refs[:per]
    m_ref, acc_ref = refs[per : per + 2]
    z0 = info_ref[NZ]
    q_iota = lax.broadcasted_iota(jnp.int32, (TROWS, 1), 0)
    q_rel = (q_iota // 8) * 64 + q_iota % 8 + z0 * 8
    if chunk == 0:
        every = edges_of(info_ref, kv_refs)
        for g in range(NG):
            for i in range(3):
                refs[per + 2][g, i] = every[g][i]
    else:
        every = [[edge_in[g, i] for i in range(3)] for g in range(NG)]
    inner = every[chunk * GC : (chunk + 1) * GC]

    def tiles(u, carry):
        count_of = None
        for j in range(JOIN):
            t = u * JOIN + j
            first_pos = t * TILE_POS + z0 * 8
            for g in range(GC):
                low = doc_start(first_pos, inner[g]) // BLOCK_POS
                need = (t + 1) * TILE_BLOCKS - low
                count_of = need if count_of is None else jnp.maximum(count_of, need)

        def work(count):
            rows = count * BLOCK_ROWS
            width = -(-per * rows // 128) * 128
            col = lax.broadcasted_iota(jnp.int32, (1, width), 1)
            inside, k_z = col, jnp.full_like(col, info_ref[0])
            for i in range(1, per):
                inside = jnp.where(col >= i * rows, col - i * rows, inside)
                k_z = jnp.where(col >= i * rows, info_ref[i], k_z)
            k_rel = (inside // 8) * 64 + inside % 8 + k_z * 8
            k_rel = jnp.where(col >= per * rows, 1 << 20, k_rel)
            pad = [jnp.zeros((width - per * rows, HD), jnp.bfloat16)] * (width > per * rows)
            items, scores, vals = [], [], []
            for j in range(JOIN):
                t = u * JOIN + j
                row0 = pl.multiple_of(t * TROWS, TROWS)
                block = jnp.maximum((t + 1) * TILE_BLOCKS - count, 0)
                for g in range(GC):
                    q_tile = q_ref[chunk * GC + g, :, pl.ds(row0, TROWS), :]
                    k0 = pl.multiple_of(g * KROWS + block * BLOCK_ROWS, BLOCK_ROWS)
                    at = pl.ds(k0, rows)
                    keys = jnp.concatenate([r[at, :HD] for r in kv_refs] + pad, axis=0)
                    val = jnp.concatenate([r[at, HD:] for r in kv_refs] + pad, axis=0)
                    vals.append(jnp.concatenate([val, jnp.ones_like(val)], axis=1))
                    s = lax.dot_general(
                        q_tile.reshape(GS * TROWS, HD),
                        keys,
                        (((1,), (1,)), ((), ())),
                        preferred_element_type=jnp.float32,
                    )
                    k_pos = block * BLOCK_POS + k_rel
                    q_pos = t * TILE_POS + q_rel
                    ok = (k_pos <= q_pos) & (k_pos >= doc_start(q_pos, inner[g]))
                    bias = jnp.where(ok, 0.0, NEG)
                    scores.append(s.reshape(GS, TROWS, width) + bias[None])
                    items.append((g, row0))
            tops = [jnp.max(s, axis=-1, keepdims=True) for s in scores]
            weights = [
                jnp.exp2((s - m) * SCALE).astype(jnp.bfloat16).reshape(GS * TROWS, width)
                for s, m in zip(scores, tops)
            ]
            outs = [
                jnp.dot(w, v, preferred_element_type=jnp.float32) for w, v in zip(weights, vals)
            ]
            for (g, row0), top, out in zip(items, tops, outs):
                at = pl.ds(row0, TROWS)
                acc_ref[g, :, at, :] = out.reshape(GS, TROWS, 2 * HD)
                m_ref[g, :, at, :] = jnp.broadcast_to(top, (GS, TROWS, HD))

        for count in range(TILE_BLOCKS, MAXB + 1):
            pl.when(count_of == count)(functools.partial(work, count))
        return carry

    lax.fori_loop(0, NT // JOIN, tiles, 0)


def far_kernel(info_ref, edge_ref, q_ref, *refs):
    m_refs, acc_refs, kv_refs = (refs[i * CHUNKS : (i + 1) * CHUNKS] for i in range(3))
    o_ref = refs[3 * CHUNKS]
    r_iota = lax.broadcasted_iota(jnp.int32, (KROWS, 1), 0)
    c_iota = lax.broadcasted_iota(jnp.int32, (1, KROWS), 1)
    q_pos = (r_iota // 8) * 64 + r_iota % 8 + info_ref[NZ] * 8
    k_pos = (c_iota // 8) * 64 + c_iota % 8 + info_ref[NZ - 1] * 8
    for g in range(NG):
        q_start = doc_start(q_pos, [edge_ref[g, i] for i in range(3)])
        bias = jnp.where((k_pos <= q_pos) & (k_pos >= q_start), 0.0, NEG)
        at = pl.ds(g % GC * KROWS, KROWS)
        keys, val = kv_refs[g // GC][at, :HD], kv_refs[g // GC][at, HD:]
        val = jnp.concatenate([val, jnp.ones_like(val)], axis=1)
        for hh in range(GS):
            s = lax.dot_general(
                q_ref[g, hh], keys, (((1,), (1,)), ((), ())), preferred_element_type=jnp.float32
            )
            s = s + bias
            before = m_refs[g // GC][g % GC, hh]
            m = jnp.maximum(before, jnp.max(s, axis=-1, keepdims=True))
            w = jnp.exp2((s - jnp.concatenate([m, m], axis=1)) * SCALE).astype(jnp.bfloat16)
            out = jnp.dot(w, val, preferred_element_type=jnp.float32)
            fade = jnp.exp2((before - m) * SCALE)
            acc = acc_refs[g // GC][g % GC, hh]
            num = acc[:, :HD] * fade + out[:, :HD]
            den = acc[:, HD:] * fade + out[:, HD:]
            o_ref[:, g, :, hh * HD : (hh + 1) * HD] = (
                (num / den).reshape(NSY, ROWS, HD).astype(jnp.bfloat16)
            )


def attention_near(chunk, info, edges, q, kvs):
    smem = pl.BlockSpec(memory_space=pltpu.SMEM)
    vmem = pl.BlockSpec(memory_space=pltpu.VMEM)
    out_shape = [
        jax.ShapeDtypeStruct((GC, GS, KROWS, HD), jnp.float32),
        jax.ShapeDtypeStruct((GC, GS, KROWS, 2 * HD), jnp.float32),
    ]
    out_specs = [vmem, vmem]
    if chunk == 0:
        out_shape.append(jax.ShapeDtypeStruct((NG, 3), jnp.int32))
        out_specs.append(smem)
    return pl.pallas_call(
        functools.partial(near_kernel, chunk),
        out_shape=out_shape,
        in_specs=[smem, smem] + [vmem] * (1 + len(kvs)),
        out_specs=out_specs,
        compiler_params=pltpu.CompilerParams(vmem_limit_bytes=24 * 1024 * 1024),
        cost_estimate=pl.CostEstimate(
            flops=800_000_000, bytes_accessed=10_000_000, transcendentals=2_000_000
        ),
        name="attention_near",
    )(info, edges, q, *kvs)


def attention_far(info, edges, q, *kvs):
    smem = pl.BlockSpec(memory_space=pltpu.SMEM)
    vmem = pl.BlockSpec(memory_space=pltpu.VMEM)
    return pl.pallas_call(
        far_kernel,
        out_shape=jax.ShapeDtypeStruct((NSY, NG, ROWS, GS * HD), jnp.bfloat16),
        in_specs=[smem, smem] + [vmem] * (1 + len(kvs)),
        out_specs=vmem,
        compiler_params=pltpu.CompilerParams(vmem_limit_bytes=24 * 1024 * 1024),
        cost_estimate=pl.CostEstimate(
            flops=800_000_000, bytes_accessed=7_000_000, transcendentals=1_500_000
        ),
        name="attention_far",
    )(info, edges, q, *kvs)


def whole(kernel, mib, out_shape, *args):
    return pl.pallas_call(
        kernel,
        out_shape=out_shape,
        compiler_params=pltpu.CompilerParams(vmem_limit_bytes=mib * 1024 * 1024),
        name=kernel.__name__,
    )(*args)


def swap(value, axes):
    return lax.all_to_all(value, axes, split_axis=0, concat_axis=0, tiled=True)


def along_z(value, step):
    return lax.ppermute(value, "z", [(i, (i + step) % NZ) for i in range(NZ)])


def on_device(queries, keys, values, slot_order, doc_ids):
    slot = slot_order[0]
    bf16 = jnp.bfloat16
    z0 = lax.axis_index("z")

    vmem, anywhere = pl.BlockSpec(memory_space=pltpu.VMEM), pl.BlockSpec(memory_space=pl.ANY)
    kv_out = pl.pallas_call(
        kv_send_kernel,
        out_shape=jax.ShapeDtypeStruct((2, KVH, 2, 32, 2 * HD), bf16),
        in_specs=[vmem, anywhere, anywhere],
        out_specs=vmem,
        scratch_shapes=[
            pltpu.VMEM((2, 128, KVH * HD), bf16),
            pltpu.SemaphoreType.DMA((2,)),
        ],
        compiler_params=pltpu.CompilerParams(vmem_limit_bytes=60 * 1024 * 1024),
        name="kv_send_kernel",
    )(slot, keys, values)
    q_out = whole(q_send_kernel, 24, jax.ShapeDtypeStruct((2, KVH, 2, 32, GS * HD), bf16), slot, queries)
    kv = swap(kv_out.reshape(NSY, 32, 2 * HD), PLANE)
    _, doc_ids = lax.optimization_barrier((kv_out, doc_ids))
    edge = whole(edge_kernel, 24, jax.ShapeDtypeStruct((16, HD), bf16), doc_ids)
    part = jax.ShapeDtypeStruct((GC * KROWS + 16, 2 * HD), bf16)
    up = list(whole(ring_kernel, 24, (part,) * CHUNKS, kv, edge, along_z(edge, NZ // 2)))
    down = list(up)
    have = [[one] for one in up]
    for step in range(NZ // 2 - 1):
        for c in range(CHUNKS):
            up[c] = along_z(up[c], 1)
            down[c] = along_z(down[c], -1)
            have[c] += [up[c], down[c]]
    _, q_out = lax.optimization_barrier((have[0][0], q_out))
    q = swap(q_out.reshape(NSY, 32, GS * HD), PLANE)
    q = q.reshape(NSY, NG, ROWS, GS, HD).transpose(1, 3, 0, 2, 4).reshape(NG, GS, KROWS, HD)

    offsets = [0, -1, 1, -2, 2, -3, 3, 4]
    places = [(z0 + o + NZ) % NZ for o in offsets]
    info = jnp.stack(places + [z0, lax.axis_index("yh") * NG]).astype(jnp.int32)
    last = [along_z(up[0], 1), along_z(down[1], -1)]
    m0, acc0, edges = attention_near(0, info, info[None], q, have[0])
    m1, acc1 = attention_near(1, info, edges, q, have[1])
    out = attention_far(info, edges, q, m0, m1, acc0, acc1, *last)
    got = swap(out.reshape(NSY, NG * ROWS, GS * HD), PLANE)
    got = got.reshape(2, KVH, 2, NG * ROWS, GS * HD)
    vmem = pl.BlockSpec(memory_space=pltpu.VMEM)
    return pl.pallas_call(
        put_back_kernel,
        out_shape=jax.ShapeDtypeStruct((128, QH * HD), bf16),
        in_specs=[vmem, vmem],
        out_specs=pl.BlockSpec(memory_space=pltpu.HBM),
        scratch_shapes=[pltpu.VMEM((128, QH * HD), bf16), pltpu.SemaphoreType.DMA((KVH,))],
        compiler_params=pltpu.CompilerParams(vmem_limit_bytes=24 * 1024 * 1024),
        name="put_back",
    )(slot, got)


def solution(mesh):
    fine = Mesh(mesh.devices.reshape(2, NZ, 2, 4, 2), ("yl", "z", "yh", "x", "c"))
    rows = P(("yl", "z", "yh", "x", "c"), None)
    return jax.shard_map(
        on_device,
        mesh=fine,
        in_specs=(rows, rows, rows, P(("yl", "z"), ("yh", "x", "c"), None), P(("yl", "z"), None)),
        out_specs=rows,
        check_vma=False,
    )
```
